32 devices in a mesh: mem: 2 (over core), state: 16 (over z, y, x).
Axes of the slice: x: 2, y: 2, z: 4, core: 2. Of those that a mesh axis runs over, the one named last changes fastest.
Arguments:
- background_ensemble: bfloat16 [80, 1048576], P('mem', 'state'), may hold values from -6 to 6
- measured_segment_index: int32 [2, 256], replicated, may hold values from 0 to 31
- measured_place_within_segment: int32 [2, 256], replicated, may hold values from 0 to 32767
- measured_readings: float32 [2, 256], replicated, may hold values from -6 to 6
- measured_noise_spread: float32 [2, 256], replicated, may hold values from 0.25 to 4
- measured_damping_weight: float32 [2, 256], replicated, may hold values from 0.3 to 1
- measured_cutoff_extent: int32 [2, 256], replicated, may hold values from 1 to 1024
Outputs:
- analysis: bfloat16 [80, 1048576], P('mem', 'state')
The draws below stay inside these ranges and needn't reach their ends.
Inputs may be any that keep to these rules, and one draw needn't show every extreme that they name: measured_segment_index numbers the blocks of 32768 state values in the order of the state dimension. measured_place_within_segment is a position inside the owner's block.
All inputs are finite; a program needn't handle non-finite values.
Results may differ from the reference program's by a relative error of at most 0.0051.
Values may be sent and summed in bfloat16 or wider, within the bound.
A program may use at most 64 MiB of HBM per device.

```python
import math
import jax
import jax.numpy as jnp
import numpy as np
from jax import lax

ENSEMBLE_COUNT = 80
SD = 32768
K = 256
B = 2
LB = 128
BLK = 4096
GRID_UNKNOWNS = 1048576
N_MEM = 2
N_STATE = 16


def place_ends(drawn, rng, low, high):
    extent = drawn.shape
    index_at = [jax.random.randint(jax.random.fold_in(rng, axis), (), 0, extent[axis]) for axis in range(len(extent))]
    drawn = drawn.at[tuple(index_at)].set(low)
    longest = extent.index(max(extent))
    index_at[longest] = (index_at[longest] + 1) % extent[longest]
    return drawn.at[tuple(index_at)].set(high)


def block_levels(stream_key, shape, split, low, top_value):
    def one(axis_at, blocks):
        draws = jax.random.uniform(jax.random.fold_in(jax.random.fold_in(stream_key, 6), axis_at), (blocks,), jnp.float32, low / len(split), top_value / len(split))
        return jnp.repeat(jnp.exp(draws), shape[axis_at] // blocks).reshape((-1,) + (1,) * (len(shape) - axis_at - 1))

    loudness = one(*split[0])
    for cut in split[1:]:
        loudness = loudness * one(*cut)
    return loudness


def cumulative_ranks(count, skew):
    weights = [(1 << 20) // math.isqrt(standing ** skew) + 1 for standing in range(1, count + 1)]
    spread = 1 + sum(weights) // (1 << 30)
    return np.cumsum(np.array([max(1, weight // spread) for weight in weights]))


def ranked_ids(stream_key, extent, number_of, slope):
    grid = cumulative_ranks(number_of, slope)
    lot = jax.random.randint(jax.random.fold_in(stream_key, 1), extent, 0, int(grid[number_of - 1]))
    standing = jnp.searchsorted(jnp.asarray(grid, jnp.int32), lot, side="right")
    return jax.random.permutation(jax.random.fold_in(stream_key, 2), number_of)[standing].astype(jnp.int32)


def normal_values(own_key, extent, scale, reach, cuts=(), held_as=jnp.bfloat16):
    result = jax.random.normal(own_key, extent, jnp.float32) * scale
    if len(cuts) > 0:
        result = block_levels(own_key, extent, cuts, -0.22, 0.18) * result
    return jnp.clip(result, min=-reach, max=reach).astype(held_as)


def setup_inputs(seed: int = 0) -> dict:
    seeds = jax.random.split(jax.random.key(seed), 8)
    return {
        "background_ensemble": normal_values(seeds[0], (ENSEMBLE_COUNT, GRID_UNKNOWNS), 1.0, 6.0, ((0, 2), (1, 16))),
        "measured_segment_index": place_ends(ranked_ids(seeds[1], (B, K), N_MEM * N_STATE, 2), jax.random.fold_in(seeds[1], 3), 0, (N_MEM * N_STATE) - 1).astype(jnp.int32),
        "measured_place_within_segment": place_ends(jax.random.randint(seeds[2], (B, K), 0, SD), jax.random.fold_in(seeds[2], 1), 0, SD - 1).astype(jnp.int32),
        "measured_readings": normal_values(seeds[3], (B, K), 1.5, 6.0, (), jnp.float32),
        "measured_noise_spread": jnp.clip(jnp.exp(jax.random.uniform(seeds[4], (B, K), jnp.float32, math.log(0.25), math.log(4.0))), 0.25, 4.0),
        "measured_damping_weight": jnp.clip(jax.random.uniform(seeds[5], (B, K), jnp.float32, 0.3, 1.0), 0.3, 1.0),
        "measured_cutoff_extent": place_ends(jax.random.randint(seeds[6], (B, K), 1, 4 * SD // LB + 1), jax.random.fold_in(seeds[6], 1), 1, (4 * SD // LB + 1) - 1).astype(jnp.int32),
    }


def observe_stats(prior_ens, values, variances):
    centre = lax.optimization_barrier(jnp.mean(prior_ens, axis=0))
    anomaly = prior_ens - centre
    prior_var = lax.optimization_barrier(jnp.sum(anomaly * anomaly, axis=0)) / (ENSEMBLE_COUNT - 1) + 1e-06
    post_var = 1.0 / (1.0 / prior_var + 1.0 / variances)
    post_mean = post_var * (centre / prior_var + values / variances)
    shrink = jnp.sqrt(post_var / prior_var)
    increment = (post_mean - centre + (shrink - 1.0) * anomaly).astype(jnp.bfloat16)
    scaling = 1.0 / ((ENSEMBLE_COUNT - 1) * prior_var)
    return (increment, anomaly.astype(jnp.bfloat16), scaling)

def taper_weights(columns, obs_index, taper_row, reach_row):
    distance = jnp.abs(columns[:, None] // LB - obs_index[None, :] // LB).astype(jnp.float32)
    return taper_row[None, :] * jnp.maximum(0.0, 1.0 - distance / (reach_row[None, :].astype(jnp.float32) + 1.0))

def update_block(block_values, columns, obs_index, taper_row, reach_row, increment, anomaly, scaling):
    values = block_values.astype(jnp.float32)
    centred = (values - lax.optimization_barrier(jnp.mean(values, axis=0))).astype(jnp.bfloat16)
    covariance = lax.dot_general(centred, anomaly, (((0,), (0,)), ((), ())), preferred_element_type=jnp.float32)
    gain_matrix = (taper_weights(columns, obs_index, taper_row, reach_row) * covariance * scaling[None, :]).astype(jnp.bfloat16)
    change = lax.dot_general(increment, gain_matrix, (((1,), (1,)), ((), ())), preferred_element_type=jnp.float32)
    return (values + change).astype(jnp.bfloat16)

def reference(background_ensemble, measured_segment_index, measured_place_within_segment, measured_readings, measured_noise_spread, measured_damping_weight, measured_cutoff_extent):
    realization_vectors = background_ensemble
    total_cols = realization_vectors.shape[1]
    for batch_no in range(B):
        obs_index = (measured_segment_index[batch_no] * SD + measured_place_within_segment[batch_no]).astype(jnp.int32)
        prior_ens = jnp.take(realization_vectors, obs_index, axis=1).astype(jnp.float32)
        increment, anomaly, scaling = observe_stats(prior_ens, measured_readings[batch_no], measured_noise_spread[batch_no])
        current = realization_vectors
        taper_row = measured_damping_weight[batch_no]
        reach_row = measured_cutoff_extent[batch_no]

        def per_block(block_no):
            start_col = (block_no * BLK).astype(jnp.int32)
            block_values = lax.dynamic_slice_in_dim(current, start_col, BLK, 1)
            columns = start_col + jnp.arange(BLK, dtype=jnp.int32)
            return update_block(block_values, columns, obs_index, taper_row, reach_row, increment, anomaly, scaling)
        updated = lax.map(per_block, jnp.arange(total_cols // BLK, dtype=jnp.int32))
        realization_vectors = jnp.transpose(updated, (1, 0, 2)).reshape(realization_vectors.shape[0], total_cols)
    return realization_vectors
```

```python
import functools

import jax
import jax.numpy as jnp
from jax import lax
from jax.experimental import pallas as pl
from jax.experimental.pallas import tpu as pltpu
from jax.sharding import PartitionSpec as P

ENSEMBLE_COUNT = 80
SD = 32768
K = 256
B = 2
LB = 128
CHUNK = 2048
DEPTH = 128
BF = jnp.bfloat16
F32 = jnp.float32


def pick_kernel(slab_ref, seg_ref, place_ref, x_ref, out_ref):
    members, width = x_ref.shape
    base = slab_ref[0] * width
    lanes = lax.broadcasted_iota(jnp.int32, (members, LB), 1)
    for group in range(B * K // LB):
        batch, first = divmod(group * LB, K)

        def step(i, acc):
            column = seg_ref[batch, first + i] * SD + place_ref[batch, first + i] - base
            held = (column >= 0) & (column < width)
            column = jnp.clip(column, 0, width - 1)
            start = pl.multiple_of((column >> 7) * LB, LB)
            block = x_ref[:, pl.ds(start, LB)].astype(F32)
            turned = pltpu.roll(block, (i - (column & (LB - 1)) + LB) & (LB - 1), 1)
            return jnp.where(lanes == jnp.where(held, i, -1), turned, acc)

        acc = lax.fori_loop(0, LB, step, jnp.zeros((members, LB), F32), unroll=8)
        out_ref[:, group * LB : (group + 1) * LB] = acc.astype(out_ref.dtype)


def stats(prior, values, variances):
    centre = jnp.sum(prior, axis=0, keepdims=True) / ENSEMBLE_COUNT
    anomaly = prior - centre
    prior_var = jnp.sum(anomaly * anomaly, axis=0, keepdims=True) / (ENSEMBLE_COUNT - 1) + 1e-06
    post_var = 1.0 / (1.0 / prior_var + 1.0 / variances)
    post_mean = post_var * (centre / prior_var + values / variances)
    shrink = jnp.sqrt(post_var / prior_var)
    increment = (post_mean - centre + (shrink - 1.0) * anomaly).astype(BF)
    return increment, anomaly, 1.0 / ((ENSEMBLE_COUNT - 1) * prior_var)


def deep(values):
    rows, columns = values.shape
    return jnp.concatenate([values, jnp.zeros((DEPTH - rows, columns), F32)], axis=0)


def centred_of(values):
    return deep(values - jnp.sum(values, axis=0, keepdims=True) / ENSEMBLE_COUNT).astype(BF)


def members_last(anomaly):
    turned = jnp.transpose(deep(anomaly))
    return turned.astype(BF)


def dot(a, b):
    return jnp.dot(a, b, preferred_element_type=F32)


def update_kernel(
    slab_ref, seg_ref, place_ref, reading_ref, noise_ref, damp_ref, cutoff_ref,
    mine_ref, other_ref, x_ref, y_ref, out_ref, inc1, inc2, anom1, anom2, rows,
):
    step = pl.program_id(0)
    own = x_ref.shape[0]
    blocks = x_ref.shape[1] // LB

    @pl.when(step == 0)
    def _():
        prior = jnp.concatenate([mine_ref[...].astype(F32), other_ref[...].astype(F32)], axis=0)
        place = [(seg_ref[b : b + 1] * SD + place_ref[b : b + 1]) // LB for b in range(B)]
        place = [p.astype(F32) for p in place]
        reach = [1.0 / (cutoff_ref[b : b + 1].astype(F32) + 1.0) for b in range(B)]
        damp = [damp_ref[b : b + 1] for b in range(B)]
        first, a, scale = stats(prior[:, :K], reading_ref[0:1], noise_ref[0:1])
        anom1[...] = members_last(a)
        inc1[...] = first.astype(F32)
        side = jnp.concatenate([damp[0] * scale, place[0], reach[0], jnp.zeros((DEPTH - 3, K), F32)], axis=0)
        side = jnp.transpose(side)
        later = prior[:, K:]
        covariance = dot(anom1[...], centred_of(later))
        taper = jnp.maximum(0.0, 1.0 - jnp.abs(place[1] - side[:, 1:2]) * side[:, 2:3])
        gain = (side[:, 0:1] * taper * covariance).astype(BF)
        later = (later + dot(first, gain)).astype(BF).astype(F32)
        second, a, scale2 = stats(later, reading_ref[1:2], noise_ref[1:2])
        anom2[...] = members_last(a)
        inc2[...] = second.astype(F32)[:own]
        rows[...] = jnp.concatenate(
            [damp[0] * scale, place[0], reach[0], damp[1] * scale2, place[1], reach[1], jnp.zeros((2, K), F32)],
            axis=0,
        )

    base = (slab_ref[0] * pl.num_programs(0) + step) * blocks

    def scaled(increment, at, block):
        away = jnp.abs((base + block).astype(F32) - rows[at + 1 : at + 2])
        return increment * (rows[at : at + 1] * jnp.maximum(0.0, 1.0 - away * rows[at + 2 : at + 3]))

    left1, left2 = inc1[...], inc2[...]
    every = left1.shape[0]
    group = 8
    for low in range(0, blocks, group):
        some = range(low, low + group)
        t1 = dot(jnp.concatenate([scaled(left1, 0, b) for b in some], axis=0).astype(BF), anom1[...])
        t2 = dot(jnp.concatenate([scaled(left2, 3, b) for b in some], axis=0).astype(BF), anom2[...])
        for n, b in enumerate(some):
            at = slice(b * LB, (b + 1) * LB)
            values = jnp.concatenate([x_ref[:, at].astype(F32), y_ref[:, at].astype(F32)], axis=0)
            change = dot(t1[n * every : (n + 1) * every].astype(BF), centred_of(values))
            values = (values + change).astype(BF).astype(F32)
            change = dot(t2[n * own : (n + 1) * own].astype(BF), centred_of(values))
            out_ref[:, at] = (values[:own] + change).astype(BF)


def on_device(x, segment, place, readings, noise, damping, cutoff):
    members, width = x.shape
    slab = lax.axis_index("state").astype(jnp.int32).reshape(1)
    swap = [(0, 1), (1, 0)]
    y = lax.ppermute(x, "mem", swap)
    smem = pl.BlockSpec(memory_space=pltpu.SMEM)
    vmem = pl.BlockSpec(memory_space=pltpu.VMEM)
    mine = pl.pallas_call(
        pick_kernel,
        out_shape=jax.ShapeDtypeStruct((members, B * K), BF),
        in_specs=[smem, smem, smem, vmem],
        out_specs=vmem,
        compiler_params=pltpu.CompilerParams(vmem_limit_bytes=16 * 2**20),
        cost_estimate=pl.CostEstimate(flops=10**7, bytes_accessed=x.size * 2, transcendentals=0),
        name="pick",
    )(slab, segment, place, x)
    size = lax.axis_size("state")
    hop = 1
    while hop < size:
        mine = mine + lax.ppermute(mine, "state", [(i, i ^ hop) for i in range(size)])
        hop *= 2
    other = lax.ppermute(mine, "mem", swap)
    whole = lambda a: pl.BlockSpec(a.shape, lambda i: (0, 0))
    part = pl.BlockSpec((members, CHUNK), lambda i: (0, i))
    small = [segment, place, readings, noise, damping, cutoff, mine, other]
    return pl.pallas_call(
        update_kernel,
        grid=(width // CHUNK,),
        out_shape=jax.ShapeDtypeStruct(x.shape, x.dtype),
        in_specs=[smem] + [whole(a) for a in small] + [part, part],
        out_specs=part,
        scratch_shapes=[
            pltpu.VMEM((2 * members, K), F32),
            pltpu.VMEM((members, K), F32),
            pltpu.VMEM((K, DEPTH), BF),
            pltpu.VMEM((K, DEPTH), BF),
            pltpu.VMEM((8, K), F32),
        ],
        compiler_params=pltpu.CompilerParams(vmem_limit_bytes=32 * 2**20),
        cost_estimate=pl.CostEstimate(flops=width * 4 * 10**5, bytes_accessed=x.size * 6, transcendentals=0),
        name="update",
    )(slab, *small, x, y)


def solution(mesh):
    placed = (P("mem", "state"), P(), P(), P(), P(), P(), P())
    return jax.shard_map(
        on_device, mesh=mesh, in_specs=placed, out_specs=P("mem", "state"), check_vma=False
    )
```

```python
import functools

import jax
import jax.numpy as jnp
from jax import lax
from jax.experimental import pallas as pl
from jax.experimental.pallas import tpu as pltpu
from jax.sharding import PartitionSpec as P

ENSEMBLE_COUNT = 80
SD = 32768
K = 256
B = 2
LB = 128
CHUNK = 4096
GROUP = 16
DEPTH = 128
BF = jnp.bfloat16
F32 = jnp.float32


def pick_kernel(slab_ref, seg_ref, place_ref, x_ref, out_ref):
    members, width = x_ref.shape
    base = slab_ref[0] * width
    lanes = lax.broadcasted_iota(jnp.int32, (members, LB), 1)
    for group in range(B * K // LB):
        batch, first = divmod(group * LB, K)

        def step(i, acc):
            column = seg_ref[batch, first + i] * SD + place_ref[batch, first + i] - base
            held = (column >= 0) & (column < width)
            column = jnp.clip(column, 0, width - 1)
            start = pl.multiple_of((column >> 7) * LB, LB)
            block = x_ref[:, pl.ds(start, LB)].astype(F32)
            turned = pltpu.roll(block, (i - (column & (LB - 1)) + LB) & (LB - 1), 1)
            return jnp.where(lanes == jnp.where(held, i, -1), turned, acc)

        acc = lax.fori_loop(0, LB, step, jnp.zeros((members, LB), F32), unroll=8)
        out_ref[:, group * LB : (group + 1) * LB] = acc.astype(out_ref.dtype)


def stats(prior, values, variances):
    centre = jnp.sum(prior, axis=0, keepdims=True) / ENSEMBLE_COUNT
    anomaly = prior - centre
    prior_var = jnp.sum(anomaly * anomaly, axis=0, keepdims=True) / (ENSEMBLE_COUNT - 1) + 1e-06
    post_var = 1.0 / (1.0 / prior_var + 1.0 / variances)
    post_mean = post_var * (centre / prior_var + values / variances)
    shrink = jnp.sqrt(post_var / prior_var)
    increment = (post_mean - centre + (shrink - 1.0) * anomaly).astype(BF)
    return increment, anomaly, 1.0 / ((ENSEMBLE_COUNT - 1) * prior_var)


def deep(values):
    rows, columns = values.shape
    return jnp.concatenate([values, jnp.zeros((DEPTH - rows, columns), F32)], axis=0)


def centred_of(values):
    return deep(values - jnp.sum(values, axis=0, keepdims=True) / ENSEMBLE_COUNT).astype(BF)


def members_last(anomaly):
    turned = jnp.transpose(deep(anomaly))
    return turned.astype(BF)


def dot(a, b):
    return jnp.dot(a, b, preferred_element_type=F32)


def update_kernel(
    slab_ref, seg_ref, place_ref, reading_ref, noise_ref, damp_ref, cutoff_ref,
    mine_ref, other_ref, x_ref, y_ref, out_ref, inc1, inc2, anom1, right, rows,
):
    step = pl.program_id(0)
    own = x_ref.shape[0]
    blocks = x_ref.shape[1] // LB

    @pl.when(step == 0)
    def _():
        prior = jnp.concatenate([mine_ref[...].astype(F32), other_ref[...].astype(F32)], axis=0)
        place = [(seg_ref[b : b + 1] * SD + place_ref[b : b + 1]) // LB for b in range(B)]
        place = [p.astype(F32) for p in place]
        reach = [1.0 / (cutoff_ref[b : b + 1].astype(F32) + 1.0) for b in range(B)]
        damp = [damp_ref[b : b + 1] for b in range(B)]
        first, a, scale = stats(prior[:, :K], reading_ref[0:1], noise_ref[0:1])
        anom1[...] = members_last(a)
        increment = first.astype(F32)
        inc1[...] = increment[:own]
        side = jnp.concatenate([damp[0] * scale, place[0], reach[0], jnp.zeros((DEPTH - 3, K), F32)], axis=0)
        side = jnp.transpose(side)
        later = prior[:, K:]
        covariance = dot(anom1[...], centred_of(later))
        taper = jnp.maximum(0.0, 1.0 - jnp.abs(place[1] - side[:, 1:2]) * side[:, 2:3])
        gain = (side[:, 0:1] * taper * covariance).astype(BF)
        later = (later + dot(first, gain)).astype(BF).astype(F32)
        second, a, scale2 = stats(later, reading_ref[1:2], noise_ref[1:2])
        anom2 = members_last(a)
        right[:, :K] = dot(anom2, centred_of(increment)).astype(BF)
        right[:, K:] = anom2
        inc2[...] = second.astype(F32)[:own]
        rows[...] = jnp.concatenate(
            [damp[0] * scale, place[0], reach[0], damp[1] * scale2, place[1], reach[1], jnp.zeros((2, K), F32)],
            axis=0,
        )

    base = (slab_ref[0] * pl.num_programs(0) + step) * blocks

    def weight(at, block):
        away = jnp.abs((base + block).astype(F32) - rows[at + 1 : at + 2])
        return rows[at : at + 1] * jnp.maximum(0.0, 1.0 - away * rows[at + 2 : at + 3])

    left1, left2 = inc1[...], inc2[...]
    none = jnp.zeros((own, DEPTH), F32)
    for low in range(0, blocks, GROUP):
        some = range(low, low + GROUP)
        both = dot(jnp.concatenate([left2 * weight(3, b) for b in some], axis=0).astype(BF), right[...])
        first = [
            (left1 + both[n * own : (n + 1) * own, :K]) * weight(0, b) for n, b in enumerate(some)
        ]
        matrix = both[:, K:] + dot(jnp.concatenate(first, axis=0).astype(BF), anom1[...])
        for n in range(0, GROUP, 2):
            pair = [slice((low + n + i) * LB, (low + n + i + 1) * LB) for i in (0, 1)]
            mine = [x_ref[:, at].astype(F32) for at in pair]
            deeps = [
                centred_of(jnp.concatenate([m, y_ref[:, at].astype(F32)], axis=0))
                for m, at in zip(mine, pair)
            ]
            upper = jnp.concatenate([matrix[n * own : (n + 1) * own], none], axis=1)
            lower = jnp.concatenate([none, matrix[(n + 1) * own : (n + 2) * own]], axis=1)
            change = dot(
                jnp.concatenate([upper, lower], axis=0).astype(BF), jnp.concatenate(deeps, axis=0)
            )
            for i in (0, 1):
                out_ref[:, pair[i]] = (mine[i] + change[i * own : (i + 1) * own]).astype(BF)


def on_device(x, segment, place, readings, noise, damping, cutoff):
    members, width = x.shape
    slab = lax.axis_index("state").astype(jnp.int32).reshape(1)
    swap = [(0, 1), (1, 0)]
    y = lax.ppermute(x, "mem", swap)
    smem = pl.BlockSpec(memory_space=pltpu.SMEM)
    vmem = pl.BlockSpec(memory_space=pltpu.VMEM)
    mine = pl.pallas_call(
        pick_kernel,
        out_shape=jax.ShapeDtypeStruct((members, B * K), BF),
        in_specs=[smem, smem, smem, vmem],
        out_specs=vmem,
        compiler_params=pltpu.CompilerParams(vmem_limit_bytes=16 * 2**20),
        cost_estimate=pl.CostEstimate(flops=10**7, bytes_accessed=x.size * 2, transcendentals=0),
        name="pick",
    )(slab, segment, place, x)
    size = lax.axis_size("state")
    hop = 1
    while hop < size:
        mine = mine + lax.ppermute(mine, "state", [(i, i ^ hop) for i in range(size)])
        hop *= 2
    other = lax.ppermute(mine, "mem", swap)
    whole = lambda a: pl.BlockSpec(a.shape, lambda i: (0, 0))
    part = pl.BlockSpec((members, CHUNK), lambda i: (0, i))
    small = [segment, place, readings, noise, damping, cutoff, mine, other]
    return pl.pallas_call(
        update_kernel,
        grid=(width // CHUNK,),
        out_shape=jax.ShapeDtypeStruct(x.shape, x.dtype),
        in_specs=[smem] + [whole(a) for a in small] + [part, part],
        out_specs=part,
        scratch_shapes=[
            pltpu.VMEM((members, K), F32),
            pltpu.VMEM((members, K), F32),
            pltpu.VMEM((K, DEPTH), BF),
            pltpu.VMEM((K, K + DEPTH), BF),
            pltpu.VMEM((8, K), F32),
        ],
        compiler_params=pltpu.CompilerParams(vmem_limit_bytes=32 * 2**20),
        cost_estimate=pl.CostEstimate(flops=width * 4 * 10**5, bytes_accessed=x.size * 6, transcendentals=0),
        name="update",
    )(slab, *small, x, y)


def solution(mesh):
    placed = (P("mem", "state"), P(), P(), P(), P(), P(), P())
    return jax.shard_map(
        on_device, mesh=mesh, in_specs=placed, out_specs=P("mem", "state"), check_vma=False
    )
```

```python
import functools

import jax
import jax.numpy as jnp
from jax import lax
from jax.experimental import pallas as pl
from jax.experimental.pallas import tpu as pltpu
from jax.sharding import PartitionSpec as P

ENSEMBLE_COUNT = 80
SD = 32768
K = 256
B = 2
LB = 128
CHUNK = 4096
GROUP = 16
DEPTH = 128
BF = jnp.bfloat16
F32 = jnp.float32
MESH = pl.DeviceIdType.MESH


def pick_kernel(slab_ref, seg_ref, place_ref, x_ref, out_ref):
    members, width = x_ref.shape
    base = slab_ref[0] * width
    lanes = lax.broadcasted_iota(jnp.int32, (members, LB), 1)
    for group in range(B * K // LB):
        batch, first = divmod(group * LB, K)

        def step(i, acc):
            column = seg_ref[batch, first + i] * SD + place_ref[batch, first + i] - base
            held = (column >= 0) & (column < width)
            column = jnp.clip(column, 0, width - 1)
            start = pl.multiple_of((column >> 7) * LB, LB)
            block = x_ref[:, pl.ds(start, LB)].astype(F32)
            turned = pltpu.roll(block, (i - (column & (LB - 1)) + LB) & (LB - 1), 1)
            return jnp.where(lanes == jnp.where(held, i, -1), turned, acc)

        acc = lax.fori_loop(0, LB, step, jnp.zeros((members, LB), F32), unroll=8)
        acc = jnp.concatenate([acc, jnp.zeros((out_ref.shape[0] - members, LB), F32)], axis=0)
        out_ref[:, group * LB : (group + 1) * LB] = acc.astype(out_ref.dtype)


def share_kernel(radices, own_ref, mine_ref, other_ref, sums, slots, send_sem, recv_sem, swap_sem):
    me = lax.axis_index("state")
    sibling = {"mem": 1 - lax.axis_index("mem")}
    partners, stride = [], 1
    for radix in radices:
        digit = (me // stride) % radix
        partners.append(
            [{"state": me + ((digit + r) % radix - digit) * stride} for r in range(1, radix)]
        )
        stride *= radix
    barrier = pltpu.get_barrier_semaphore()
    every = [p for stage in partners for p in stage] + [sibling]
    for partner in every:
        pl.semaphore_signal(barrier, inc=1, device_id=partner, device_id_type=MESH)
    pl.semaphore_wait(barrier, len(every))

    for stage, group in enumerate(partners):
        source = own_ref if stage == 0 else sums.at[stage - 1]
        copies = [
            pltpu.make_async_remote_copy(
                src_ref=source,
                dst_ref=slots.at[stage, r],
                send_sem=send_sem.at[stage, r],
                recv_sem=recv_sem.at[stage, r],
                device_id=partner,
                device_id_type=MESH,
            )
            for r, partner in enumerate(group)
        ]
        for copy in copies:
            copy.start()
        total = source[...].astype(F32)
        for copy in copies:
            copy.wait()
        for r in range(len(group)):
            total = total + slots[stage, r].astype(F32)
        sums[stage] = total.astype(BF)
    last = sums.at[len(partners) - 1]
    copy = pltpu.make_async_remote_copy(
        src_ref=last,
        dst_ref=slots.at[len(partners), 0],
        send_sem=swap_sem.at[0],
        recv_sem=swap_sem.at[1],
        device_id=sibling,
        device_id_type=MESH,
    )
    copy.start()
    mine_ref[...] = last[...]
    copy.wait()
    other_ref[...] = slots[len(partners), 0]


def stats(prior, values, variances):
    centre = jnp.sum(prior, axis=0, keepdims=True) / ENSEMBLE_COUNT
    anomaly = prior - centre
    prior_var = jnp.sum(anomaly * anomaly, axis=0, keepdims=True) / (ENSEMBLE_COUNT - 1) + 1e-06
    post_var = 1.0 / (1.0 / prior_var + 1.0 / variances)
    post_mean = post_var * (centre / prior_var + values / variances)
    shrink = jnp.sqrt(post_var / prior_var)
    increment = (post_mean - centre + (shrink - 1.0) * anomaly).astype(BF)
    return increment, anomaly, 1.0 / ((ENSEMBLE_COUNT - 1) * prior_var)


def deep(values):
    rows, columns = values.shape
    return jnp.concatenate([values, jnp.zeros((DEPTH - rows, columns), F32)], axis=0)


def centred_of(values):
    return deep(values - jnp.sum(values, axis=0, keepdims=True) / ENSEMBLE_COUNT).astype(BF)


def members_last(anomaly):
    turned = jnp.transpose(deep(anomaly))
    return turned.astype(BF)


def dot(a, b):
    return jnp.dot(a, b, preferred_element_type=F32)


def update_kernel(
    slab_ref, seg_ref, place_ref, reading_ref, noise_ref, damp_ref, cutoff_ref,
    mine_ref, other_ref, x_ref, y_ref, out_ref, inc1, inc2, anom1, right, rows,
):
    step = pl.program_id(0)
    own = x_ref.shape[0]
    blocks = x_ref.shape[1] // LB

    @pl.when(step == 0)
    def _():
        prior = jnp.concatenate(
            [mine_ref[...].astype(F32)[:own], other_ref[...].astype(F32)[:own]], axis=0
        )
        place = [(seg_ref[b : b + 1] * SD + place_ref[b : b + 1]) // LB for b in range(B)]
        place = [p.astype(F32) for p in place]
        reach = [1.0 / (cutoff_ref[b : b + 1].astype(F32) + 1.0) for b in range(B)]
        damp = [damp_ref[b : b + 1] for b in range(B)]
        first, a, scale = stats(prior[:, :K], reading_ref[0:1], noise_ref[0:1])
        anom1[...] = members_last(a)
        increment = first.astype(F32)
        inc1[...] = increment[:own]
        side = jnp.concatenate([damp[0] * scale, place[0], reach[0], jnp.zeros((DEPTH - 3, K), F32)], axis=0)
        side = jnp.transpose(side)
        later = prior[:, K:]
        covariance = dot(anom1[...], centred_of(later))
        taper = jnp.maximum(0.0, 1.0 - jnp.abs(place[1] - side[:, 1:2]) * side[:, 2:3])
        gain = (side[:, 0:1] * taper * covariance).astype(BF)
        later = (later + dot(first, gain)).astype(BF).astype(F32)
        second, a, scale2 = stats(later, reading_ref[1:2], noise_ref[1:2])
        anom2 = members_last(a)
        right[:, :K] = dot(anom2, centred_of(increment)).astype(BF)
        right[:, K:] = anom2
        inc2[...] = second.astype(F32)[:own]
        rows[...] = jnp.concatenate(
            [damp[0] * scale, place[0], reach[0], damp[1] * scale2, place[1], reach[1], jnp.zeros((2, K), F32)],
            axis=0,
        )

    base = (slab_ref[0] * pl.num_programs(0) + step) * blocks

    def weight(at, block):
        away = jnp.abs((base + block).astype(F32) - rows[at + 1 : at + 2])
        return rows[at : at + 1] * jnp.maximum(0.0, 1.0 - away * rows[at + 2 : at + 3])

    left1, left2 = inc1[...], inc2[...]
    none = jnp.zeros((own, DEPTH), F32)
    for low in range(0, blocks, GROUP):
        some = range(low, low + GROUP)
        both = dot(jnp.concatenate([left2 * weight(3, b) for b in some], axis=0).astype(BF), right[...])
        first = [
            (left1 + both[n * own : (n + 1) * own, :K]) * weight(0, b) for n, b in enumerate(some)
        ]
        matrix = both[:, K:] + dot(jnp.concatenate(first, axis=0).astype(BF), anom1[...])
        for n in range(0, GROUP, 2):
            pair = [slice((low + n + i) * LB, (low + n + i + 1) * LB) for i in (0, 1)]
            mine = [x_ref[:, at].astype(F32) for at in pair]
            deeps = [
                centred_of(jnp.concatenate([m, y_ref[:, at].astype(F32)], axis=0))
                for m, at in zip(mine, pair)
            ]
            upper = jnp.concatenate([matrix[n * own : (n + 1) * own], none], axis=1)
            lower = jnp.concatenate([none, matrix[(n + 1) * own : (n + 2) * own]], axis=1)
            change = dot(
                jnp.concatenate([upper, lower], axis=0).astype(BF), jnp.concatenate(deeps, axis=0)
            )
            for i in (0, 1):
                out_ref[:, pair[i]] = (mine[i] + change[i * own : (i + 1) * own]).astype(BF)


def on_device(x, segment, place, readings, noise, damping, cutoff):
    members, width = x.shape
    slab = lax.axis_index("state").astype(jnp.int32).reshape(1)
    swap = [(0, 1), (1, 0)]
    y = lax.ppermute(x, "mem", swap)
    smem = pl.BlockSpec(memory_space=pltpu.SMEM)
    vmem = pl.BlockSpec(memory_space=pltpu.VMEM)
    mine = pl.pallas_call(
        pick_kernel,
        out_shape=jax.ShapeDtypeStruct((-(-members // 16) * 16, B * K), BF),
        in_specs=[smem, smem, smem, vmem],
        out_specs=vmem,
        compiler_params=pltpu.CompilerParams(vmem_limit_bytes=16 * 2**20),
        cost_estimate=pl.CostEstimate(flops=10**7, bytes_accessed=x.size * 2, transcendentals=0),
        name="pick",
    )(slab, segment, place, x)
    size, radices = lax.axis_size("state"), []
    while size > 1:
        radices.append(4 if size % 4 == 0 else size)
        size //= radices[-1]
    stages, most = len(radices), max(radices) - 1
    shared = jax.ShapeDtypeStruct(mine.shape, BF)
    mine, other = pl.pallas_call(
        functools.partial(share_kernel, radices),
        out_shape=[shared, shared],
        in_specs=[vmem],
        out_specs=[vmem, vmem],
        scratch_shapes=[
            pltpu.VMEM((stages,) + mine.shape, BF),
            pltpu.VMEM((stages + 1, most) + mine.shape, BF),
            pltpu.SemaphoreType.DMA((stages, most)),
            pltpu.SemaphoreType.DMA((stages, most)),
            pltpu.SemaphoreType.DMA((2,)),
        ],
        compiler_params=pltpu.CompilerParams(
            collective_id=0, has_side_effects=True, vmem_limit_bytes=8 * 2**20
        ),
        cost_estimate=pl.CostEstimate(flops=10**6, bytes_accessed=10**6, transcendentals=0),
        name="share",
    )(mine)
    whole = lambda a: pl.BlockSpec(a.shape, lambda i: (0, 0))
    part = pl.BlockSpec((members, CHUNK), lambda i: (0, i))
    small = [segment, place, readings, noise, damping, cutoff, mine, other]
    return pl.pallas_call(
        update_kernel,
        grid=(width // CHUNK,),
        out_shape=jax.ShapeDtypeStruct(x.shape, x.dtype),
        in_specs=[smem] + [whole(a) for a in small] + [part, part],
        out_specs=part,
        scratch_shapes=[
            pltpu.VMEM((members, K), F32),
            pltpu.VMEM((members, K), F32),
            pltpu.VMEM((K, DEPTH), BF),
            pltpu.VMEM((K, K + DEPTH), BF),
            pltpu.VMEM((8, K), F32),
        ],
        compiler_params=pltpu.CompilerParams(vmem_limit_bytes=32 * 2**20),
        cost_estimate=pl.CostEstimate(flops=width * 4 * 10**5, bytes_accessed=x.size * 6, transcendentals=0),
        name="update",
    )(slab, *small, x, y)


def solution(mesh):
    placed = (P("mem", "state"), P(), P(), P(), P(), P(), P())
    return jax.shard_map(
        on_device, mesh=mesh, in_specs=placed, out_specs=P("mem", "state"), check_vma=False
    )
```

```python
import functools

import jax
import jax.numpy as jnp
from jax import lax
from jax.experimental import pallas as pl
from jax.experimental.pallas import tpu as pltpu
from jax.sharding import PartitionSpec as P

ENSEMBLE_COUNT = 80
SD = 32768
K = 256
B = 2
LB = 128
CHUNK = 4096
GROUP = 16
DEPTH = 128
BF = jnp.bfloat16
F32 = jnp.float32
MESH = pl.DeviceIdType.MESH


def pick_kernel(slab_ref, seg_ref, place_ref, x_ref, out_ref):
    members, width = x_ref.shape
    base = slab_ref[0] * width
    lanes = lax.broadcasted_iota(jnp.int32, (members, LB), 1)
    for group in range(B * K // LB):
        batch, first = divmod(group * LB, K)

        def step(i, acc):
            column = seg_ref[batch, first + i] * SD + place_ref[batch, first + i] - base
            held = (column >= 0) & (column < width)
            column = jnp.clip(column, 0, width - 1)
            start = pl.multiple_of((column >> 7) * LB, LB)
            block = x_ref[:, pl.ds(start, LB)].astype(F32)
            turned = pltpu.roll(block, (i - (column & (LB - 1)) + LB) & (LB - 1), 1)
            return jnp.where(lanes == jnp.where(held, i, -1), turned, acc)

        acc = lax.fori_loop(0, LB, step, jnp.zeros((members, LB), F32), unroll=32)
        acc = jnp.concatenate([acc, jnp.zeros((out_ref.shape[0] - members, LB), F32)], axis=0)
        out_ref[:, group * LB : (group + 1) * LB] = acc.astype(out_ref.dtype)


def share_kernel(radices, own_ref, mine_ref, other_ref, sums, slots, send_sem, recv_sem, swap_sem):
    me = lax.axis_index("state")
    sibling = {"mem": 1 - lax.axis_index("mem")}
    partners, stride = [], 1
    for radix in radices:
        digit = (me // stride) % radix
        partners.append(
            [{"state": me + ((digit + r) % radix - digit) * stride} for r in range(1, radix)]
        )
        stride *= radix
    barrier = pltpu.get_barrier_semaphore()
    every = [p for stage in partners for p in stage] + [sibling]
    for partner in every:
        pl.semaphore_signal(barrier, inc=1, device_id=partner, device_id_type=MESH)
    pl.semaphore_wait(barrier, len(every))

    for stage, group in enumerate(partners):
        source = own_ref if stage == 0 else sums.at[stage - 1]
        copies = [
            pltpu.make_async_remote_copy(
                src_ref=source,
                dst_ref=slots.at[stage, r],
                send_sem=send_sem.at[stage, r],
                recv_sem=recv_sem.at[stage, r],
                device_id=partner,
                device_id_type=MESH,
            )
            for r, partner in enumerate(group)
        ]
        for copy in copies:
            copy.start()
        total = source[...].astype(F32)
        for copy in copies:
            copy.wait()
        for r in range(len(group)):
            total = total + slots[stage, r].astype(F32)
        sums[stage] = total.astype(BF)
    last = sums.at[len(partners) - 1]
    copy = pltpu.make_async_remote_copy(
        src_ref=last,
        dst_ref=slots.at[len(partners), 0],
        send_sem=swap_sem.at[0],
        recv_sem=swap_sem.at[1],
        device_id=sibling,
        device_id_type=MESH,
    )
    copy.start()
    mine_ref[...] = last[...]
    copy.wait()
    other_ref[...] = slots[len(partners), 0]


def stats(prior, values, variances):
    centre = jnp.sum(prior, axis=0, keepdims=True) / ENSEMBLE_COUNT
    anomaly = prior - centre
    prior_var = jnp.sum(anomaly * anomaly, axis=0, keepdims=True) / (ENSEMBLE_COUNT - 1) + 1e-06
    post_var = 1.0 / (1.0 / prior_var + 1.0 / variances)
    post_mean = post_var * (centre / prior_var + values / variances)
    shrink = jnp.sqrt(post_var / prior_var)
    increment = (post_mean - centre + (shrink - 1.0) * anomaly).astype(BF)
    return increment, anomaly, 1.0 / ((ENSEMBLE_COUNT - 1) * prior_var)


def deep(values):
    rows, columns = values.shape
    return jnp.concatenate([values, jnp.zeros((DEPTH - rows, columns), F32)], axis=0)


def centred_of(values):
    return deep(values - jnp.sum(values, axis=0, keepdims=True) / ENSEMBLE_COUNT).astype(BF)


def members_last(anomaly):
    turned = jnp.transpose(deep(anomaly))
    return turned.astype(BF)


def dot(a, b):
    return jnp.dot(a, b, preferred_element_type=F32)


def update_kernel(
    slab_ref, seg_ref, place_ref, reading_ref, noise_ref, damp_ref, cutoff_ref,
    mine_ref, other_ref, x_ref, y_ref, out_ref, inc1, inc2, anom1, right, rows,
):
    step = pl.program_id(0)
    own = x_ref.shape[0]
    blocks = x_ref.shape[1] // LB

    @pl.when(step == 0)
    def _():
        prior = jnp.concatenate(
            [mine_ref[...].astype(F32)[:own], other_ref[...].astype(F32)[:own]], axis=0
        )
        place = [(seg_ref[b : b + 1] * SD + place_ref[b : b + 1]) // LB for b in range(B)]
        place = [p.astype(F32) for p in place]
        reach = [1.0 / (cutoff_ref[b : b + 1].astype(F32) + 1.0) for b in range(B)]
        damp = [damp_ref[b : b + 1] for b in range(B)]
        first, a, scale = stats(prior[:, :K], reading_ref[0:1], noise_ref[0:1])
        anom1[...] = members_last(a)
        increment = first.astype(F32)
        inc1[...] = increment[:own]
        side = jnp.concatenate([damp[0] * scale, place[0], reach[0], jnp.zeros((DEPTH - 3, K), F32)], axis=0)
        side = jnp.transpose(side)
        later = prior[:, K:]
        covariance = dot(anom1[...], centred_of(later))
        taper = jnp.maximum(0.0, 1.0 - jnp.abs(place[1] - side[:, 1:2]) * side[:, 2:3])
        gain = (side[:, 0:1] * taper * covariance).astype(BF)
        later = (later + dot(first, gain)).astype(BF).astype(F32)
        second, a, scale2 = stats(later, reading_ref[1:2], noise_ref[1:2])
        anom2 = members_last(a)
        right[:, :K] = dot(anom2, centred_of(increment)).astype(BF)
        right[:, K:] = anom2
        inc2[...] = second.astype(F32)[:own]
        rows[...] = jnp.concatenate(
            [damp[0] * scale, place[0], reach[0], damp[1] * scale2, place[1], reach[1], jnp.zeros((2, K), F32)],
            axis=0,
        )

    base = (slab_ref[0] * pl.num_programs(0) + step) * blocks

    def weight(at, block):
        away = jnp.abs((base + block).astype(F32) - rows[at + 1 : at + 2])
        return rows[at : at + 1] * jnp.maximum(0.0, 1.0 - away * rows[at + 2 : at + 3])

    left1, left2 = inc1[...], inc2[...]
    none = jnp.zeros((own, DEPTH), F32)
    for low in range(0, blocks, GROUP):
        some = range(low, low + GROUP)
        both = dot(jnp.concatenate([left2 * weight(3, b) for b in some], axis=0).astype(BF), right[...])
        first = [
            (left1 + both[n * own : (n + 1) * own, :K]) * weight(0, b) for n, b in enumerate(some)
        ]
        matrix = both[:, K:] + dot(jnp.concatenate(first, axis=0).astype(BF), anom1[...])
        for n in range(0, GROUP, 2):
            pair = [slice((low + n + i) * LB, (low + n + i + 1) * LB) for i in (0, 1)]
            mine = [x_ref[:, at].astype(F32) for at in pair]
            deeps = [
                centred_of(jnp.concatenate([m, y_ref[:, at].astype(F32)], axis=0))
                for m, at in zip(mine, pair)
            ]
            upper = jnp.concatenate([matrix[n * own : (n + 1) * own], none], axis=1)
            lower = jnp.concatenate([none, matrix[(n + 1) * own : (n + 2) * own]], axis=1)
            change = dot(
                jnp.concatenate([upper, lower], axis=0).astype(BF), jnp.concatenate(deeps, axis=0)
            )
            for i in (0, 1):
                out_ref[:, pair[i]] = (mine[i] + change[i * own : (i + 1) * own]).astype(BF)


def on_device(x, segment, place, readings, noise, damping, cutoff):
    members, width = x.shape
    slab = lax.axis_index("state").astype(jnp.int32).reshape(1)
    swap = [(0, 1), (1, 0)]
    y = lax.ppermute(x, "mem", swap)
    smem = pl.BlockSpec(memory_space=pltpu.SMEM)
    vmem = pl.BlockSpec(memory_space=pltpu.VMEM)
    mine = pl.pallas_call(
        pick_kernel,
        out_shape=jax.ShapeDtypeStruct((-(-members // 16) * 16, B * K), BF),
        in_specs=[smem, smem, smem, vmem],
        out_specs=vmem,
        compiler_params=pltpu.CompilerParams(vmem_limit_bytes=16 * 2**20),
        cost_estimate=pl.CostEstimate(flops=10**7, bytes_accessed=x.size * 2, transcendentals=0),
        name="pick",
    )(slab, segment, place, x)
    size, radices = lax.axis_size("state"), []
    while size > 1:
        radices.append(4 if size % 4 == 0 else size)
        size //= radices[-1]
    stages, most = len(radices), max(radices) - 1
    shared = jax.ShapeDtypeStruct(mine.shape, BF)
    mine, other = pl.pallas_call(
        functools.partial(share_kernel, radices),
        out_shape=[shared, shared],
        in_specs=[vmem],
        out_specs=[vmem, vmem],
        scratch_shapes=[
            pltpu.VMEM((stages,) + mine.shape, BF),
            pltpu.VMEM((stages + 1, most) + mine.shape, BF),
            pltpu.SemaphoreType.DMA((stages, most)),
            pltpu.SemaphoreType.DMA((stages, most)),
            pltpu.SemaphoreType.DMA((2,)),
        ],
        compiler_params=pltpu.CompilerParams(
            collective_id=0, has_side_effects=True, vmem_limit_bytes=8 * 2**20
        ),
        cost_estimate=pl.CostEstimate(flops=10**6, bytes_accessed=10**6, transcendentals=0),
        name="share",
    )(mine)
    whole = lambda a: pl.BlockSpec(a.shape, lambda i: (0, 0))
    part = pl.BlockSpec((members, CHUNK), lambda i: (0, i))
    small = [segment, place, readings, noise, damping, cutoff, mine, other]
    return pl.pallas_call(
        update_kernel,
        grid=(width // CHUNK,),
        out_shape=jax.ShapeDtypeStruct(x.shape, x.dtype),
        in_specs=[smem] + [whole(a) for a in small] + [part, part],
        out_specs=part,
        scratch_shapes=[
            pltpu.VMEM((members, K), F32),
            pltpu.VMEM((members, K), F32),
            pltpu.VMEM((K, DEPTH), BF),
            pltpu.VMEM((K, K + DEPTH), BF),
            pltpu.VMEM((8, K), F32),
        ],
        compiler_params=pltpu.CompilerParams(vmem_limit_bytes=32 * 2**20),
        cost_estimate=pl.CostEstimate(flops=width * 4 * 10**5, bytes_accessed=x.size * 6, transcendentals=0),
        name="update",
    )(slab, *small, x, y)


def solution(mesh):
    placed = (P("mem", "state"), P(), P(), P(), P(), P(), P())
    return jax.shard_map(
        on_device, mesh=mesh, in_specs=placed, out_specs=P("mem", "state"), check_vma=False
    )
```
